256 devices in a mesh: leaf: 32 (over z, x), orb: 8 (over y, core).
Axes of the slice: x: 4, y: 4, z: 8, core: 2. Of those that a mesh axis runs over, the one named last changes fastest.
Arguments:
- orbitals: bfloat16 [160, 256, 16, 256], P('leaf', 'orb')
- potential: bfloat16 [160, 16, 256], P('leaf'), may hold values from 0.29882812 to 2
- counts: int32 [32], replicated, may hold values from 1 to 5, as said below
- neighbour_owner: int32 [160, 6], P('leaf'), may hold values from -1 to 31, as said below
- neighbour_slot: int32 [160, 6], P('leaf'), may hold values from 0 to 4, as said below
- pair_factor: bfloat16 [7, 256, 4, 256], replicated, may hold values from -0.0625 to 0.0625
- axis_factor: bfloat16 [7, 4, 16, 16], replicated, may hold values from -1.5 to 1.5
Outputs:
- rotated: bfloat16 [160, 256, 16, 256], P('leaf', 'orb')
The draws below stay inside these ranges and needn't reach their ends.
Inputs may be any that keep to these rules, and one draw needn't show every extreme that they name: `counts`: counts of live boxes per subtree; they sum to 3 times the number of subtrees, and some subtree holds 5. `neighbour_owner`: for a live slot on subtree p the neighbour lies on subtree p - 1, p or p + 1, or is absent (-1); empty slots hold -1 everywhere. `neighbour_slot`: A neighbour points to a live slot; on the subtree below it is one of that subtree's last min(2, count) live slots, on the subtree above one of its first min(2, count) slots, and both ends of this range are used in every draw; absent neighbours hold 0.
All inputs are finite; a program needn't handle non-finite values.
Results may differ from the reference program's by a relative error of at most 0.0013.
The reference program's roundings to bfloat16 on the way count: a program that leaves them out, or rounds other values in their place, can miss the bound.
Values may be sent and summed in bfloat16 or wider, within the bound.
A program may use at most 128 MiB of HBM per device.

```python
import math
import jax
import jax.numpy as jnp
from jax import lax

K = 16
PAIR = 256
ORBS = 256
TERMS = 4
EDGE = 2
BOX_DEV = 3
SLOTS = 5
TOTAL = 160
N_LEAF = 32


def layout_tables(key):
    base = jax.random.fold_in(key, 11)
    key_perm, key_moves, key_kind, key_pick = jax.random.split(base, 4)
    order = jax.random.permutation(key_perm, N_LEAF)
    half = N_LEAF // 2
    spread = SLOTS - BOX_DEV
    moves = jax.random.randint(key_moves, (half,), 0, spread + 1).astype(jnp.int32)
    moves = moves.at[0].set(spread)
    shifts = jnp.zeros((N_LEAF,), jnp.int32).at[order[:half]].add(moves).at[order[half:]].add(-moves)
    counts = (BOX_DEV + shifts).astype(jnp.int32)
    slot_ids = jnp.arange(TOTAL, dtype=jnp.int32)
    device = slot_ids // SLOTS
    within = slot_ids % SLOTS
    live_mask = within < counts[device]
    lower = jnp.clip(device - 1, 0, N_LEAF - 1)
    upper = jnp.clip(device + 1, 0, N_LEAF - 1)
    count_here = counts[device][:, None]
    count_low = counts[lower][:, None]
    count_up = counts[upper][:, None]
    kinds = jax.random.randint(key_kind, (TOTAL, 6), 0, 9).astype(jnp.int32)
    picks = jax.random.randint(key_pick, (TOTAL, 6), 0, 1 << 20).astype(jnp.int32)
    has_low = (device > 0)[:, None]
    has_up = (device < N_LEAF - 1)[:, None]
    column = device[:, None]
    wants_low = (kinds >= 4) & (kinds <= 6) & has_low
    wants_up = (kinds >= 7) & has_up
    owner = jnp.where(wants_low, column - 1, jnp.where(wants_up, column + 1, column))
    local_slot = picks % count_here
    low_slot = count_low - 1 - picks % jnp.minimum(EDGE, count_low)
    up_slot = picks % jnp.minimum(EDGE, count_up)
    slot_val = jnp.where(wants_low, low_slot, jnp.where(wants_up, up_slot, local_slot))
    owner = jnp.where(kinds == 0, -1, owner)
    slot_val = jnp.where(kinds == 0, 0, slot_val)
    busiest = order[0]
    below_end = busiest < N_LEAF - 1
    row_forced = jnp.where(below_end, (busiest + 1) * SLOTS, (busiest - 1) * SLOTS)
    col_forced = jnp.where(below_end, 0, 1)
    slot_forced = jnp.where(below_end, SLOTS - EDGE, EDGE - 1)
    owner = owner.at[row_forced, col_forced].set(busiest)
    slot_val = slot_val.at[row_forced, col_forced].set(slot_forced)
    other_row = jnp.where(below_end, (busiest + 1) * SLOTS, (busiest - 1) * SLOTS)
    other_col = jnp.where(below_end, 2, 3)
    other_slot = jnp.where(below_end, SLOTS - 1, 0)
    owner = owner.at[other_row, other_col].set(busiest)
    slot_val = slot_val.at[other_row, other_col].set(other_slot)
    owner = jnp.where(live_mask[:, None], owner, -1).astype(jnp.int32)
    slot_val = jnp.where(live_mask[:, None], slot_val, 0).astype(jnp.int32)
    return (counts, owner, slot_val)


def draw_counts(key, part):
    return layout_tables(key)[0]


def draw_neighbour_owner(key, part):
    return layout_tables(key)[1]


def draw_neighbour_slot(key, part):
    return layout_tables(key)[2]


def draw_orbitals(key, part):
    base = jax.random.fold_in(key, 23)
    key_scale, key_main = jax.random.split(base, 2)
    shape = (TOTAL, ORBS, K, PAIR)
    scales = jnp.exp(jax.random.uniform(key_scale, (1, ORBS, 1, 1), jnp.float32, 0.0, math.log(3.5)))
    values = jax.random.normal(key_main, shape, jnp.float32) * scales
    return values.astype(jnp.bfloat16)


def steps_of(own_key, dims, pieces, low, top_value):
    def one(axis_at, parts):
        steps = jax.random.uniform(jax.random.fold_in(jax.random.fold_in(own_key, 6), axis_at), (parts,), jnp.float32, low / len(pieces), top_value / len(pieces))
        return jnp.repeat(jnp.exp(steps), dims[axis_at] // parts).reshape((-1,) + (1,) * (len(dims) - axis_at - 1))

    loudness = one(*pieces[0])
    for cut in pieces[1:]:
        loudness = loudness * one(*cut)
    return loudness


def bell_draw(own_key, extent, scale, reach, kind=jnp.bfloat16):
    return jnp.clip(scale * jax.random.normal(own_key, extent, jnp.float32), -reach, reach).astype(kind)


def setup_inputs(seed: int = 0) -> dict:
    seeds = jax.random.split(jax.random.key(seed), 8)
    return {
        "orbitals": draw_orbitals(jax.random.fold_in(seeds[7], 71), 0),
        "potential": jnp.clip(0.29882812 + 1.7011719 * jax.random.uniform(seeds[1], (TOTAL, K, PAIR), jnp.float32) ** steps_of(seeds[1], (TOTAL, K, PAIR), ((0, 32),), -0.2, 0.2), 0.29882812, 2.0).astype(jnp.bfloat16),
        "counts": draw_counts(jax.random.fold_in(seeds[7], 71), 0),
        "neighbour_owner": draw_neighbour_owner(jax.random.fold_in(seeds[7], 71), 0),
        "neighbour_slot": draw_neighbour_slot(jax.random.fold_in(seeds[7], 71), 0),
        "pair_factor": bell_draw(seeds[5], (7, PAIR, TERMS, PAIR), (7 * TERMS * PAIR) ** -0.5, 0.0625),
        "axis_factor": bell_draw(seeds[6], (7, TERMS, K, K), K ** -0.5, 1.5),
    }


def reference(orbitals, potential, counts, neighbour_owner, neighbour_slot, pair_factor, axis_factor):
    product = (orbitals.astype(jnp.float32) * potential[:, None].astype(jnp.float32)).astype(jnp.bfloat16)
    padded = jnp.concatenate([product, jnp.zeros((1,) + product.shape[1:], jnp.bfloat16)], axis=0)
    slot_ids = jnp.arange(TOTAL, dtype=jnp.int32)
    owners = slot_ids // SLOTS
    live_mask = slot_ids % SLOTS < counts[owners]
    targets = jnp.where(neighbour_owner >= 0, neighbour_owner * SLOTS + neighbour_slot, TOTAL).astype(jnp.int32)
    orb_count = orbitals.shape[1]

    def propagate(box):
        sources = [padded[targets[box, d]] for d in range(6)] + [product[box]]
        total = jnp.zeros((orb_count, K, PAIR), jnp.float32)
        for direction in range(7):
            flat = sources[direction].reshape(orb_count * K, PAIR)
            inner = jnp.dot(flat, pair_factor[direction].reshape(PAIR, TERMS * PAIR), preferred_element_type=jnp.float32)
            inner = inner.astype(jnp.bfloat16).reshape(orb_count, K, TERMS, PAIR)
            total = total + jnp.einsum('bzrp,rzw->bwp', inner.astype(jnp.float32), axis_factor[direction].astype(jnp.float32))
        return jnp.where(live_mask[box], total, 0.0).astype(jnp.bfloat16)
    propagated = lax.map(propagate, slot_ids)

    def add_intersection(carry, block):
        flat = block.reshape(orb_count, K * PAIR)
        return (carry + jnp.dot(flat, flat.T, preferred_element_type=jnp.float32), None)
    intersection, unused = lax.scan(add_intersection, jnp.zeros((orb_count, orb_count), jnp.float32), propagated)
    scale = jnp.trace(intersection) / ORBS
    identity = jnp.eye(orb_count, dtype=jnp.float32)
    rotation = ((1.5 * identity - 0.5 * intersection / scale) / jnp.sqrt(scale)).astype(jnp.bfloat16)

    def rotate(block):
        flat = block.reshape(orb_count, K * PAIR)
        return jnp.dot(rotation.T, flat, preferred_element_type=jnp.float32).astype(jnp.bfloat16).reshape(orb_count, K, PAIR)
    return lax.map(rotate, propagated)
```

```python
import functools

import jax
import jax.numpy as jnp
from jax import lax
from jax.experimental import pallas as pl
from jax.experimental.pallas import tpu as pltpu
from jax.sharding import PartitionSpec as P

MESH = pl.DeviceIdType.MESH
F32 = jnp.float32
BF16 = jnp.bfloat16
CO = 8


def iota(shape, dim):
    return lax.broadcasted_iota(jnp.int32, shape, dim)


def kernel(
    dims,
    counts, owner, slot, potential, axis, orbitals, pair, out_hbm,
    table, live, pair_v, staged, spread, inner, source, send1, recv1, rows_v, S, part1, part2, full,
    send2, recv2, out_v, *rest,
):
    NL, NX, NO, SL, OL, D, PP, T = dims
    NC, NZ, G = OL // CO, NL // NX, NX * NO
    ZD = D // NO
    RO = CO * D
    N = OL * NO
    PR = N // G
    pools, orb_v = rest[:NC], rest[NC:2 * NC]
    (ld_sem, pair_sem, ex_send, ex_recv, a_send, a_recv, p1_send, p1_recv, p2_send, p2_recv, p3_send, p3_recv,
     b_send, b_recv, out_sem) = rest[2 * NC:]
    me_leaf, me = lax.axis_index("leaf"), lax.axis_index("orb")
    x, z = lax.rem(me_leaf, NX), me_leaf // NX
    m = x * NO + me

    loads = [
        pltpu.make_async_copy(orbitals.at[:, c * CO:(c + 1) * CO], orb_v[c], ld_sem.at[c])
        for c in range(NC)
    ]
    pair_load = pltpu.make_async_copy(pair, pair_v, pair_sem)
    loads[0].start()
    for load in loads[1:]:
        load.start()
    pair_load.start()

    def member(q):
        return (z * NX + q // NO, lax.rem(q, NO))

    barrier = pltpu.get_barrier_semaphore()
    up, down = lax.rem(me_leaf + 1, NL), lax.rem(me_leaf + NL - 1, NL)
    pl.semaphore_signal(barrier, inc=1, device_id=(up, me), device_id_type=MESH)
    pl.semaphore_signal(barrier, inc=1, device_id=(down, me), device_id_type=MESH)

    def greet(t, carry):
        pl.semaphore_signal(barrier, inc=1, device_id=member(lax.rem(m + t, G)), device_id_type=MESH)
        return carry

    lax.fori_loop(1, G, greet, 0)

    def greet_z(t, carry):
        pl.semaphore_signal(
            barrier, inc=1, device_id=(lax.rem(z + t, NZ) * NX + x, me), device_id_type=MESH)
        return carry

    lax.fori_loop(1, NZ, greet_z, 0)

    count = counts[me_leaf]
    count_low = counts[down]
    for g in range(SL):
        live[g] = (g < count).astype(jnp.int32)
        for d in range(6):
            own, at = owner[g, d], slot[g, d]
            low = SL + jnp.clip(at - count_low + 2, 0, 1)
            high = SL + 2 + jnp.clip(at, 0, 1)
            here = jnp.clip(at, 0, SL - 1)
            place = jnp.where(own == me_leaf, here, jnp.where(own < me_leaf, low, high))
            table[d * SL + g] = jnp.where(own < 0, SL + 4, place)
        table[6 * SL + g] = g

    def make_product(c):
        loads[c].wait()

        def block(g):
            value = orb_v[c][g].astype(F32) * potential[g].astype(F32)[None]
            return value.astype(BF16).reshape(RO, PP)

        for g in range(SL):
            pools[c][g] = block(g)
        pools[c][SL + 4] = jnp.zeros((RO, PP), BF16)
        for j in range(2):
            staged[c, j] = block(jnp.maximum(count - 2 + j, 0))

    def exchange(c):
        to_up = pltpu.make_async_remote_copy(
            src_ref=staged.at[c], dst_ref=pools[c].at[SL:SL + 2], send_sem=ex_send.at[c, 0],
            recv_sem=ex_recv.at[c, 0], device_id=(up, me), device_id_type=MESH)
        to_down = pltpu.make_async_remote_copy(
            src_ref=pools[c].at[0:2], dst_ref=pools[c].at[SL + 2:SL + 4], send_sem=ex_send.at[c, 1],
            recv_sem=ex_recv.at[c, 1], device_id=(down, me), device_id_type=MESH)
        return to_up, to_down

    exchanges = [exchange(c) for c in range(NC)]

    def start_exchange(c):
        for copy in exchanges[c]:
            copy.start()

    make_product(0)
    pl.semaphore_wait(barrier, G - 1 + NZ - 1 + 2)
    start_exchange(0)
    make_product(1)
    start_exchange(1)
    for c in range(2, NC):
        make_product(c)

    shift = CO.bit_length() - 1
    rise = (iota((RO, D), 0) >> shift == iota((RO, D), 1)).astype(BF16)
    TD = T * D
    lanes = T * RO
    wide_a, wide_b = iota((TD, lanes), 0), iota((TD, lanes), 1)
    widen = ((wide_a // D == wide_b // RO) & (lax.rem(wide_a, D) == lax.rem(wide_b, D))).astype(BF16)
    same = lax.rem(iota((RO, lanes), 0), CO) == lax.rem(iota((RO, lanes), 1), RO) // D

    for d in range(7):
        tall = lax.dot_general(rise, axis[d], (((1,), (1,)), ((), ())), preferred_element_type=F32).astype(BF16)
        full_d = jnp.dot(tall, widen, preferred_element_type=F32)
        spread[:, d * lanes:(d + 1) * lanes] = jnp.where(same, full_d, 0.0).astype(BF16)

    pair_load.wait()

    def pair_step(c, d):
        for g in range(SL):
            source[g * RO:(g + 1) * RO, :] = pools[c][table[d * SL + g]]
        for r in range(T):
            value = jnp.dot(source[...], pair_v[d, r], preferred_element_type=F32).astype(BF16)
            for g in range(SL):
                inner[c % 2, g, d, r] = value[g * RO:(g + 1) * RO]

    def self_step(c):
        for r in range(T):
            own_blocks = pools[c][0:SL].reshape(SL * RO, PP)
            value = jnp.dot(own_blocks, pair_v[6, r], preferred_element_type=F32).astype(BF16)
            for g in range(SL):
                inner[c % 2, g, 6, r] = value[g * RO:(g + 1) * RO]

    def to_peer(c, t):
        peer = lax.rem(me + t, NO)
        return pltpu.make_async_remote_copy(
            src_ref=send1.at[c, peer], dst_ref=recv1.at[me, c], send_sem=a_send.at[c, peer],
            recv_sem=a_recv.at[c, me], device_id=(me_leaf, peer), device_id_type=MESH)

    def from_peer(c, t):
        peer = lax.rem(me + NO - t, NO)
        return pltpu.make_async_remote_copy(
            src_ref=send1.at[c, peer], dst_ref=recv1.at[peer, c], send_sem=a_send.at[c, peer],
            recv_sem=a_recv.at[c, peer], device_id=(me_leaf, peer), device_id_type=MESH)

    def assemble(c):
        for t in range(1, NO):
            from_peer(c, t).wait_recv()
        for g in range(SL):
            block = recv1[:, c, g * ZD * CO:(g + 1) * ZD * CO, :].astype(F32).reshape(NO, ZD, CO, PP)
            for k in range(ZD):
                rows_v[g * ZD + k, c * NO * CO:(c + 1) * NO * CO, :] = (
                    block[:, k].reshape(NO * CO, PP).astype(BF16))

    self_step(0)
    self_step(1)
    for c in range(NC):
        for copy in exchanges[c]:
            copy.wait_recv()
        if c + 2 < NC:
            start_exchange(c + 2)
        if c >= 2:
            self_step(c)

        def over_d(d, carry, c=c):
            pair_step(c, d)
            return carry

        lax.fori_loop(0, 6, over_d, 0)

        def over_g(g, carry, c=c):
            weights = inner[c % 2, g].reshape(7 * T * RO, PP)
            total = jnp.dot(spread[...], weights, preferred_element_type=F32)
            total = jnp.where(live[g] > 0, total, 0.0).astype(BF16)
            rows = ZD * CO
            for j in range(NO):
                send1[c, j, pl.ds(pl.multiple_of(g * rows, rows), rows), :] = total[j * rows:(j + 1) * rows]
            return carry

        lax.fori_loop(0, SL, over_g, 0)
        for t in range(1, NO):
            to_peer(c, t).start()
        recv1[me, c] = send1[c, me]
        if c >= 1:
            assemble(c - 1)
    assemble(NC - 1)

    total = None
    for k in range(SL * ZD):
        block = rows_v[k]
        term = lax.dot_general(block, block, (((1,), (1,)), ((), ())), preferred_element_type=F32)
        total = term if total is None else total + term
    S[...] = total

    def p1(q_from, q_to, q_dev):
        return pltpu.make_async_remote_copy(
            src_ref=S.at[pl.ds(pl.multiple_of(q_to * PR, PR), PR)], dst_ref=part1.at[q_from],
            send_sem=p1_send.at[q_dev], recv_sem=p1_recv.at[q_from], device_id=member(q_dev), device_id_type=MESH)

    def p1_start(t, carry):
        q = lax.rem(m + t, G)
        p1(m, q, q).start()
        return carry

    lax.fori_loop(1, G, p1_start, 0)
    part1[m] = S[pl.ds(pl.multiple_of(m * PR, PR), PR)]

    def p1_wait(t, carry):
        q = lax.rem(m + G - t, G)
        p1(q, q, q).wait_recv()
        return carry

    lax.fori_loop(1, G, p1_wait, 0)
    part2[z] = jnp.sum(part1[...], axis=0)

    def p2(z_from, z_to):
        return pltpu.make_async_remote_copy(
            src_ref=part2.at[z_from], dst_ref=part2.at[z_from], send_sem=p2_send.at[z_to],
            recv_sem=p2_recv.at[z_from], device_id=(z_to * NX + x, me), device_id_type=MESH)

    for t in range(1, NZ):
        p2(z, lax.rem(z + t, NZ)).start()
    for t in range(1, NZ):
        other = lax.rem(z + NZ - t, NZ)
        p2(other, other).wait_recv()
    full[m] = jnp.sum(part2[...], axis=0)

    def p3(q_from, q_dev):
        return pltpu.make_async_remote_copy(
            src_ref=full.at[q_from], dst_ref=full.at[q_from], send_sem=p3_send.at[q_dev],
            recv_sem=p3_recv.at[q_from], device_id=member(q_dev), device_id_type=MESH)

    def p3_start(t, carry):
        q = lax.rem(m + t, G)
        p3(m, q).start()
        return carry

    lax.fori_loop(1, G, p3_start, 0)

    def p3_wait(t, carry):
        q = lax.rem(m + G - t, G)
        p3(q, q).wait_recv()
        return carry

    lax.fori_loop(1, G, p3_wait, 0)

    summed = full[...].reshape(N, N)
    diagonal = iota((N, N), 0) == iota((N, N), 1)
    trace = jnp.sum(jnp.sum(jnp.where(diagonal, summed, 0.0), axis=1, keepdims=True), axis=0, keepdims=True)
    scale = trace / N
    rotation = (jnp.where(diagonal, 1.5, 0.0) - 0.5 * summed / scale) / jnp.sqrt(scale)
    turn = jnp.transpose(rotation).astype(BF16)

    def back(g, a_from, a_to):
        return pltpu.make_async_remote_copy(
            src_ref=send2.at[a_to, g], dst_ref=recv2.at[a_from, g], send_sem=b_send.at[g, a_to],
            recv_sem=b_recv.at[g, a_from], device_id=(me_leaf, a_to), device_id_type=MESH)

    for g in range(SL):
        for k in range(ZD):
            value = jnp.dot(turn, rows_v[g * ZD + k], preferred_element_type=F32).reshape(NC, NO, CO, PP)
            for s in range(NO):
                send2[s, g, k * OL:(k + 1) * OL, :] = value[:, s].reshape(OL, PP).astype(BF16)
        for t in range(1, NO):
            back(g, me, lax.rem(me + t, NO)).start()
        recv2[me, g] = send2[me, g]

    row, column = iota((D * 16, D * 16), 0), iota((D * 16, D * 16), 1)
    swap = ((row // D == lax.rem(column, 16)) & (lax.rem(row, D) == column // 16)).astype(BF16)
    stores = []
    for g in range(SL):
        for t in range(1, NO):
            other = lax.rem(me + NO - t, NO)
            back(g, other, other).wait_recv()
        for h in range(OL // 16):
            block = recv2[:, g].reshape(NO, ZD, OL // 16, 16, PP)[:, :, h].reshape(D * 16, PP)
            value = jnp.dot(swap, block, preferred_element_type=F32).astype(BF16)
            out_v[g, h * 16:(h + 1) * 16] = value.reshape(16, D, PP)
        store = pltpu.make_async_copy(out_v.at[g], out_hbm.at[g], out_sem.at[g])
        store.start()
        stores.append(store)

    for pairs in exchanges:
        for copy in pairs:
            copy.wait_send()
    for c in range(NC):
        for t in range(1, NO):
            to_peer(c, t).wait_send()

    def drain(t, carry):
        q = lax.rem(m + t, G)
        p1(m, q, q).wait_send()
        p3(m, q).wait_send()
        return carry

    lax.fori_loop(1, G, drain, 0)
    for t in range(1, NZ):
        p2(z, lax.rem(z + t, NZ)).wait_send()
    for g in range(SL):
        for t in range(1, NO):
            back(g, me, lax.rem(me + t, NO)).wait_send()
    for store in stores:
        store.wait()


def on_device(dims, orbitals, potential, counts, owner, slot, pair, axis):
    NL, NX, NO, SL, OL, D, PP, T = dims
    NC, NZ, G = OL // CO, NL // NX, NX * NO
    ZD, RO, N = D // NO, CO * D, OL * NO
    PR = N // G
    vmem = pl.BlockSpec(memory_space=pltpu.VMEM)
    smem = pl.BlockSpec(memory_space=pltpu.SMEM)
    anywhere = pl.BlockSpec(memory_space=pl.ANY)
    dma = pltpu.SemaphoreType.DMA
    pair = pair.transpose(0, 2, 1, 3)
    return pl.pallas_call(
        functools.partial(kernel, dims),
        out_shape=jax.ShapeDtypeStruct(orbitals.shape, BF16),
        in_specs=[smem, smem, smem, vmem, vmem, anywhere, anywhere],
        out_specs=anywhere,
        scratch_shapes=[
            pltpu.SMEM((7 * SL,), jnp.int32),
            pltpu.SMEM((SL,), jnp.int32),
            pltpu.VMEM((7, T, PP, PP), BF16),
            pltpu.VMEM((NC, 2, RO, PP), BF16),
            pltpu.VMEM((RO, 7 * T * RO), BF16),
            pltpu.VMEM((2, SL, 7, T, RO, PP), BF16),
            pltpu.VMEM((SL * RO, PP), BF16),
            pltpu.VMEM((NC, NO, SL * ZD * CO, PP), BF16),
            pltpu.VMEM((NO, NC, SL * ZD * CO, PP), BF16),
            pltpu.VMEM((SL * ZD, N, PP), BF16),
            pltpu.VMEM((N, N), F32),
            pltpu.VMEM((G, PR, N), F32),
            pltpu.VMEM((NZ, PR, N), F32),
            pltpu.VMEM((G, PR, N), F32),
            pltpu.VMEM((NO, SL, ZD * OL, PP), BF16),
            pltpu.VMEM((NO, SL, ZD * OL, PP), BF16),
            pltpu.VMEM((SL, OL, D, PP), BF16),
            *[pltpu.VMEM((SL + 5, RO, PP), BF16) for _ in range(NC)],
            *[pltpu.VMEM((SL, CO, D, PP), BF16) for _ in range(NC)],
            dma((NC,)), dma(()), dma((NC, 2)), dma((NC, 2)),
            dma((NC, NO)), dma((NC, NO)),
            dma((G,)), dma((G,)), dma((NZ,)), dma((NZ,)), dma((G,)), dma((G,)),
            dma((SL, NO)), dma((SL, NO)), dma((SL,)),
        ],
        compiler_params=pltpu.CompilerParams(
            collective_id=0, has_side_effects=True, vmem_limit_bytes=56 * 2**20),
    )(counts, owner, slot, potential, axis.reshape(7, T * D, D), orbitals, pair)


def solution(mesh):
    leaf, orb = mesh.shape["leaf"], mesh.shape["orb"]
    along_x = 4 if leaf % 4 == 0 and leaf > 4 else 2

    def step(orbitals, potential, counts, owner, slot, pair, axis):
        slots, orbs, depth, paired = orbitals.shape
        dims = (leaf, along_x, orb, slots, orbs, depth, paired, pair.shape[2])
        return on_device(dims, orbitals, potential, counts, owner, slot, pair, axis)

    placed = (
        P("leaf", "orb", None, None),
        P("leaf", None, None),
        P(),
        P("leaf", None),
        P("leaf", None),
        P(),
        P(),
    )
    return jax.shard_map(
        step,
        mesh=mesh,
        in_specs=placed,
        out_specs=P("leaf", "orb", None, None),
        check_vma=False,
    )
```

```python
import functools

import jax
import jax.numpy as jnp
from jax import lax
from jax.experimental import pallas as pl
from jax.experimental.pallas import tpu as pltpu
from jax.sharding import PartitionSpec as P

MESH = pl.DeviceIdType.MESH
F32 = jnp.float32
BF16 = jnp.bfloat16
CO = 8


def iota(shape, dim):
    return lax.broadcasted_iota(jnp.int32, shape, dim)


def kernel(
    dims,
    counts, owner, slot, potential, axis, orbitals, pair, recv2,
    table, live, raw_v, pair_v, staged, spread, inner, source, send1, recv1, rows_v, S, part1, part2, full,
    send2, *rest,
):
    NL, NX, NO, SL, OL, D, PP, T = dims
    NC, NZ, G = OL // CO, NL // NX, NX * NO
    ZD = D // NO
    RO = CO * D
    N = OL * NO
    PR = N // G
    pools, orb_v = rest[:NC], rest[NC:2 * NC]
    (ld_sem, pair_sem, ex_send, ex_recv, a_send, a_recv, p1_send, p1_recv, p2_send, p2_recv, p3_send, p3_recv,
     b_send, b_recv, out_sem) = rest[2 * NC:]
    me_leaf, me = lax.axis_index("leaf"), lax.axis_index("orb")
    x, z = lax.rem(me_leaf, NX), me_leaf // NX
    m = x * NO + me

    loads = [
        pltpu.make_async_copy(orbitals.at[:, c * CO:(c + 1) * CO], orb_v[c], ld_sem.at[c])
        for c in range(NC)
    ]
    pair_load = pltpu.make_async_copy(pair, raw_v, pair_sem)
    loads[0].start()
    for load in loads[1:]:
        load.start()
    pair_load.start()

    def member(q):
        return (z * NX + q // NO, lax.rem(q, NO))

    barrier = pltpu.get_barrier_semaphore()
    up, down = lax.rem(me_leaf + 1, NL), lax.rem(me_leaf + NL - 1, NL)
    pl.semaphore_signal(barrier, inc=1, device_id=(up, me), device_id_type=MESH)
    pl.semaphore_signal(barrier, inc=1, device_id=(down, me), device_id_type=MESH)

    def greet(t, carry):
        pl.semaphore_signal(barrier, inc=1, device_id=member(lax.rem(m + t, G)), device_id_type=MESH)
        return carry

    lax.fori_loop(1, G, greet, 0)

    def greet_z(t, carry):
        pl.semaphore_signal(
            barrier, inc=1, device_id=(lax.rem(z + t, NZ) * NX + x, me), device_id_type=MESH)
        return carry

    lax.fori_loop(1, NZ, greet_z, 0)

    count = counts[me_leaf]
    count_low = counts[down]
    for g in range(SL):
        live[g] = (g < count).astype(jnp.int32)
        for d in range(6):
            own, at = owner[g, d], slot[g, d]
            low = SL + jnp.clip(at - count_low + 2, 0, 1)
            high = SL + 2 + jnp.clip(at, 0, 1)
            here = jnp.clip(at, 0, SL - 1)
            place = jnp.where(own == me_leaf, here, jnp.where(own < me_leaf, low, high))
            table[d * SL + g] = jnp.where(own < 0, SL + 4, place)
        table[6 * SL + g] = g

    def make_product(c):
        loads[c].wait()

        def block(g):
            value = orb_v[c][g].astype(F32) * potential[g].astype(F32)[None]
            return value.astype(BF16).reshape(RO, PP)

        for g in range(SL):
            pools[c][g] = block(g)
        pools[c][SL + 4] = jnp.zeros((RO, PP), BF16)
        for j in range(2):
            staged[c, j] = block(jnp.maximum(count - 2 + j, 0))

    def exchange(c):
        to_up = pltpu.make_async_remote_copy(
            src_ref=staged.at[c], dst_ref=pools[c].at[SL:SL + 2], send_sem=ex_send.at[c, 0],
            recv_sem=ex_recv.at[c, 0], device_id=(up, me), device_id_type=MESH)
        to_down = pltpu.make_async_remote_copy(
            src_ref=pools[c].at[0:2], dst_ref=pools[c].at[SL + 2:SL + 4], send_sem=ex_send.at[c, 1],
            recv_sem=ex_recv.at[c, 1], device_id=(down, me), device_id_type=MESH)
        return to_up, to_down

    exchanges = [exchange(c) for c in range(NC)]

    def start_exchange(c):
        for copy in exchanges[c]:
            copy.start()

    make_product(0)
    pl.semaphore_wait(barrier, G - 1 + NZ - 1 + 2)
    start_exchange(0)
    for c in range(1, NC):
        make_product(c)

    shift = CO.bit_length() - 1
    rise = (iota((RO, D), 0) >> shift == iota((RO, D), 1)).astype(BF16)
    TD = T * D
    lanes = T * RO
    wide_a, wide_b = iota((TD, lanes), 0), iota((TD, lanes), 1)
    widen = ((wide_a // D == wide_b // RO) & (lax.rem(wide_a, D) == lax.rem(wide_b, D))).astype(BF16)
    same = lax.rem(iota((RO, lanes), 0), CO) == lax.rem(iota((RO, lanes), 1), RO) // D

    for d in range(7):
        tall = lax.dot_general(rise, axis[d], (((1,), (1,)), ((), ())), preferred_element_type=F32).astype(BF16)
        full_d = jnp.dot(tall, widen, preferred_element_type=F32)
        spread[:, d * lanes:(d + 1) * lanes] = jnp.where(same, full_d, 0.0).astype(BF16)

    pair_load.wait()
    QB = PP // T
    row, column = iota((PP, PP), 0), iota((PP, PP), 1)
    sort = ((row // QB == lax.rem(column, T)) & (lax.rem(row, QB) == column // T)).astype(BF16)
    for d in range(7):
        for q in range(0, PP, QB):
            block = jnp.dot(sort, raw_v[d, q:q + QB].reshape(PP, PP), preferred_element_type=F32).astype(BF16)
            for r in range(T):
                pair_v[d, r, q:q + QB] = block[r * QB:(r + 1) * QB]

    def pair_step(c, d):
        for g in range(SL):
            source[g * RO:(g + 1) * RO, :] = pools[c][table[d * SL + g]]
        for r in range(T):
            value = jnp.dot(source[...], pair_v[d, r], preferred_element_type=F32).astype(BF16)
            for g in range(SL):
                inner[c % 2, g, d, r] = value[g * RO:(g + 1) * RO]

    def self_step(c):
        for r in range(T):
            own_blocks = pools[c][0:SL].reshape(SL * RO, PP)
            value = jnp.dot(own_blocks, pair_v[6, r], preferred_element_type=F32).astype(BF16)
            for g in range(SL):
                inner[c % 2, g, 6, r] = value[g * RO:(g + 1) * RO]

    rows = ZD * CO

    def between(c, g, here, there, peer):
        at = pl.ds(0, SL * rows) if c < NC - 1 else pl.ds(g * rows, rows)
        return pltpu.make_async_remote_copy(
            src_ref=send1.at[c, there, at], dst_ref=recv1.at[here, c, at], send_sem=a_send.at[c + g, there],
            recv_sem=a_recv.at[c + g, here], device_id=(me_leaf, peer), device_id_type=MESH)

    def to_peer(c, t, g=0):
        peer = lax.rem(me + t, NO)
        return between(c, g, me, peer, peer)

    def from_peer(c, t, g=0):
        peer = lax.rem(me + NO - t, NO)
        return between(c, g, peer, peer, peer)

    def assemble(c):
        if c < NC - 1:
            for t in range(1, NO):
                from_peer(c, t).wait_recv()
        for g in range(SL):
            if c == NC - 1:
                for t in range(1, NO):
                    from_peer(c, t, g).wait_recv()
            block = recv1[:, c, g * rows:(g + 1) * rows, :].astype(F32).reshape(NO, ZD, CO, PP)
            for k in range(ZD):
                rows_v[g * ZD + k, c * NO * CO:(c + 1) * NO * CO, :] = (
                    block[:, k].reshape(NO * CO, PP).astype(BF16))

    start_exchange(1)
    self_step(0)
    self_step(1)
    for c in range(NC):
        for copy in exchanges[c]:
            copy.wait_recv()
        if c + 2 < NC:
            start_exchange(c + 2)
        if c >= 2:
            self_step(c)

        for d in range(6):
            pair_step(c, d)
        for g in range(SL):
            weights = inner[c % 2, g].reshape(7 * T * RO, PP)
            total = jnp.dot(spread[...], weights, preferred_element_type=F32)
            total = jnp.where(live[g] > 0, total, 0.0).astype(BF16)
            for j in range(NO):
                send1[c, j, g * rows:(g + 1) * rows, :] = total[j * rows:(j + 1) * rows]
            if c == NC - 1:
                for t in range(1, NO):
                    to_peer(c, t, g).start()
        if c < NC - 1:
            for t in range(1, NO):
                to_peer(c, t).start()
        recv1[me, c] = send1[c, me]
        if c >= 1:
            assemble(c - 1)
    assemble(NC - 1)

    total = None
    for k in range(SL * ZD):
        block = rows_v[k]
        term = lax.dot_general(block, block, (((1,), (1,)), ((), ())), preferred_element_type=F32)
        total = term if total is None else total + term
    S[...] = total

    def p1(q_from, q_to, q_dev):
        return pltpu.make_async_remote_copy(
            src_ref=S.at[pl.ds(pl.multiple_of(q_to * PR, PR), PR)], dst_ref=part1.at[q_from],
            send_sem=p1_send.at[q_dev], recv_sem=p1_recv.at[q_from], device_id=member(q_dev), device_id_type=MESH)

    def p1_start(t, carry):
        q = lax.rem(m + t, G)
        p1(m, q, q).start()
        return carry

    lax.fori_loop(1, G, p1_start, 0)
    part1[m] = S[pl.ds(pl.multiple_of(m * PR, PR), PR)]

    def p1_wait(t, carry):
        q = lax.rem(m + G - t, G)
        p1(q, q, q).wait_recv()
        return carry

    lax.fori_loop(1, G, p1_wait, 0)
    part2[z] = jnp.sum(part1[...], axis=0)

    def p2(z_from, z_to):
        return pltpu.make_async_remote_copy(
            src_ref=part2.at[z_from], dst_ref=part2.at[z_from], send_sem=p2_send.at[z_to],
            recv_sem=p2_recv.at[z_from], device_id=(z_to * NX + x, me), device_id_type=MESH)

    for t in range(1, NZ):
        p2(z, lax.rem(z + t, NZ)).start()
    for t in range(1, NZ):
        other = lax.rem(z + NZ - t, NZ)
        p2(other, other).wait_recv()
    full[m] = jnp.sum(part2[...], axis=0)

    def p3(q_from, q_dev):
        return pltpu.make_async_remote_copy(
            src_ref=full.at[q_from], dst_ref=full.at[q_from], send_sem=p3_send.at[q_dev],
            recv_sem=p3_recv.at[q_from], device_id=member(q_dev), device_id_type=MESH)

    def p3_start(t, carry):
        q = lax.rem(m + t, G)
        p3(m, q).start()
        return carry

    lax.fori_loop(1, G, p3_start, 0)

    def p3_wait(t, carry):
        q = lax.rem(m + G - t, G)
        p3(q, q).wait_recv()
        return carry

    lax.fori_loop(1, G, p3_wait, 0)

    summed = full[...].reshape(N, N)
    diagonal = iota((N, N), 0) == iota((N, N), 1)
    trace = jnp.sum(jnp.sum(jnp.where(diagonal, summed, 0.0), axis=1, keepdims=True), axis=0, keepdims=True)
    scale = trace / N
    rotation = (jnp.where(diagonal, 1.5, 0.0) - 0.5 * summed / scale) / jnp.sqrt(scale)
    turn = jnp.transpose(rotation).astype(BF16)

    def back(g, a_from, a_to):
        return pltpu.make_async_remote_copy(
            src_ref=send2.at[a_to, g], dst_ref=recv2.at[a_from, g], send_sem=b_send.at[g, a_to],
            recv_sem=b_recv.at[g, a_from], device_id=(me_leaf, a_to), device_id_type=MESH)

    keeps = []
    for g in range(SL):
        for k in range(ZD):
            value = jnp.dot(turn, rows_v[g * ZD + k], preferred_element_type=F32).reshape(NC, NO, CO, PP)
            for s in range(NO):
                send2[s, g, k * OL:(k + 1) * OL, :] = value[:, s].reshape(OL, PP).astype(BF16)
        for t in range(1, NO):
            back(g, me, lax.rem(me + t, NO)).start()
        keeps.append(pltpu.make_async_copy(send2.at[me, g], recv2.at[me, g], out_sem.at[g]))
        keeps[-1].start()

    for g in range(SL):
        for t in range(1, NO):
            other = lax.rem(me + NO - t, NO)
            back(g, other, other).wait_recv()

    for pairs in exchanges:
        for copy in pairs:
            copy.wait_send()
    for c in range(NC):
        for g in range(SL if c == NC - 1 else 1):
            for t in range(1, NO):
                to_peer(c, t, g).wait_send()

    def drain(t, carry):
        q = lax.rem(m + t, G)
        p1(m, q, q).wait_send()
        p3(m, q).wait_send()
        return carry

    lax.fori_loop(1, G, drain, 0)
    for t in range(1, NZ):
        p2(z, lax.rem(z + t, NZ)).wait_send()
    for g in range(SL):
        for t in range(1, NO):
            back(g, me, lax.rem(me + t, NO)).wait_send()
    for keep in keeps:
        keep.wait()


def settle(dims, blocks, out, held, placed, in_sem, out_sem):
    NL, NX, NO, SL, OL, D, PP, T = dims
    loads = [pltpu.make_async_copy(blocks.at[:, g], held.at[g], in_sem.at[g]) for g in range(SL)]
    stores = [pltpu.make_async_copy(placed.at[g], out.at[g], out_sem.at[g]) for g in range(SL)]
    for load in loads:
        load.start()
    row, column = iota((D * 16, D * 16), 0), iota((D * 16, D * 16), 1)
    swap = ((row // D == lax.rem(column, 16)) & (lax.rem(row, D) == column // 16)).astype(BF16)
    for g in range(SL):
        loads[g].wait()
        for h in range(OL // 16):
            block = held[g].reshape(NO, D // NO, OL // 16, 16, PP)[:, :, h].reshape(D * 16, PP)
            value = jnp.dot(swap, block, preferred_element_type=F32).astype(BF16)
            placed[g, h * 16:(h + 1) * 16] = value.reshape(16, D, PP)
        stores[g].start()
    for store in stores:
        store.wait()


def on_device(dims, orbitals, potential, counts, owner, slot, pair, axis):
    NL, NX, NO, SL, OL, D, PP, T = dims
    NC, NZ, G = OL // CO, NL // NX, NX * NO
    ZD, RO, N = D // NO, CO * D, OL * NO
    PR = N // G
    vmem = pl.BlockSpec(memory_space=pltpu.VMEM)
    smem = pl.BlockSpec(memory_space=pltpu.SMEM)
    anywhere = pl.BlockSpec(memory_space=pl.ANY)
    dma = pltpu.SemaphoreType.DMA
    blocks = pl.pallas_call(
        functools.partial(kernel, dims),
        out_shape=jax.ShapeDtypeStruct((NO, SL, ZD * OL, PP), BF16),
        in_specs=[smem, smem, smem, vmem, vmem, anywhere, anywhere],
        out_specs=anywhere,
        scratch_shapes=[
            pltpu.SMEM((7 * SL,), jnp.int32),
            pltpu.SMEM((SL,), jnp.int32),
            pltpu.VMEM((7, PP, T, PP), BF16),
            pltpu.VMEM((7, T, PP, PP), BF16),
            pltpu.VMEM((NC, 2, RO, PP), BF16),
            pltpu.VMEM((RO, 7 * T * RO), BF16),
            pltpu.VMEM((2, SL, 7, T, RO, PP), BF16),
            pltpu.VMEM((SL * RO, PP), BF16),
            pltpu.VMEM((NC, NO, SL * ZD * CO, PP), BF16),
            pltpu.VMEM((NO, NC, SL * ZD * CO, PP), BF16),
            pltpu.VMEM((SL * ZD, N, PP), BF16),
            pltpu.VMEM((N, N), F32),
            pltpu.VMEM((G, PR, N), F32),
            pltpu.VMEM((NZ, PR, N), F32),
            pltpu.VMEM((G, PR, N), F32),
            pltpu.VMEM((NO, SL, ZD * OL, PP), BF16),
            *[pltpu.VMEM((SL + 5, RO, PP), BF16) for _ in range(NC)],
            *[pltpu.VMEM((SL, CO, D, PP), BF16) for _ in range(NC)],
            dma((NC,)), dma(()), dma((NC, 2)), dma((NC, 2)),
            dma((NC - 1 + SL, NO)), dma((NC - 1 + SL, NO)),
            dma((G,)), dma((G,)), dma((NZ,)), dma((NZ,)), dma((G,)), dma((G,)),
            dma((SL, NO)), dma((SL, NO)), dma((SL,)),
        ],
        compiler_params=pltpu.CompilerParams(
            collective_id=0, has_side_effects=True, vmem_limit_bytes=56 * 2**20),
    )(counts, owner, slot, potential, axis.reshape(7, T * D, D), orbitals, pair)
    return pl.pallas_call(
        functools.partial(settle, dims),
        out_shape=jax.ShapeDtypeStruct(orbitals.shape, BF16),
        in_specs=[anywhere],
        out_specs=anywhere,
        scratch_shapes=[
            pltpu.VMEM((SL, NO, ZD * OL, PP), BF16),
            pltpu.VMEM((SL, OL, D, PP), BF16),
            dma((SL,)), dma((SL,)),
        ],
    )(blocks)


def solution(mesh):
    leaf, orb = mesh.shape["leaf"], mesh.shape["orb"]
    along_x = 4 if leaf % 4 == 0 and leaf > 4 else 2

    def step(orbitals, potential, counts, owner, slot, pair, axis):
        slots, orbs, depth, paired = orbitals.shape
        dims = (leaf, along_x, orb, slots, orbs, depth, paired, pair.shape[2])
        return on_device(dims, orbitals, potential, counts, owner, slot, pair, axis)

    placed = (
        P("leaf", "orb", None, None),
        P("leaf", None, None),
        P(),
        P("leaf", None),
        P("leaf", None),
        P(),
        P(),
    )
    return jax.shard_map(
        step,
        mesh=mesh,
        in_specs=placed,
        out_specs=P("leaf", "orb", None, None),
        check_vma=False,
    )
```

```python
import functools

import jax
import jax.numpy as jnp
from jax import lax
from jax.experimental import pallas as pl
from jax.experimental.pallas import tpu as pltpu
from jax.sharding import PartitionSpec as P

MESH = pl.DeviceIdType.MESH
F32 = jnp.float32
BF16 = jnp.bfloat16
CO = 8


def iota(shape, dim):
    return lax.broadcasted_iota(jnp.int32, shape, dim)


def split(value, size):
    return value >> (size.bit_length() - 1), value & (size - 1)


def reorder(outer, inner):
    size = outer * inner
    high, low = split(iota((size, size), 0), outer)
    other_high, other_low = split(iota((size, size), 1), inner)
    return ((high == other_low) & (low == other_high)).astype(BF16)


def kernel(
    dims,
    counts_in, owner_in, slot_in, potential_in, axis_in, orbitals, pair, recv2,
    counts, owner, slot, potential, axis, table, live, raw_v, pair_v, staged, spread, inner, source, send1, recv1, rows_v, S, part1, part2, full,
    send2, *rest,
):
    NL, NX, NO, SL, OL, D, PP, T = dims
    NC, NZ, G = OL // CO, NL // NX, NX * NO
    ZD = D // NO
    RO = CO * D
    N = OL * NO
    PR = N // G
    pools, orb_v = rest[:NC], rest[NC:2 * NC]
    (ld_sem, pair_sem, ex_send, ex_recv, a_send, a_recv, p1_send, p1_recv, p2_send, p2_recv, p3_send, p3_recv,
     b_send, b_recv, out_sem, small_sem, known) = rest[2 * NC:]
    me_leaf, me = lax.axis_index("leaf"), lax.axis_index("orb")
    x, z = lax.rem(me_leaf, NX), me_leaf // NX
    m = x * NO + me

    loads = [
        pltpu.make_async_copy(orbitals.at[:, c * CO:(c + 1) * CO], orb_v[c], ld_sem.at[c])
        for c in range(NC)
    ]
    pair_load = pltpu.make_async_copy(pair, raw_v, pair_sem)
    small = [
        pltpu.make_async_copy(*ends, small_sem.at[i])
        for i, ends in enumerate(
            ((counts_in, counts), (potential_in, potential), (owner_in, owner), (slot_in, slot), (axis_in, axis)))
    ]
    loads[0].start()
    for load in small:
        load.start()

    def member(q):
        return (z * NX + q // NO, lax.rem(q, NO))

    barrier = pltpu.get_barrier_semaphore()
    up, down = lax.rem(me_leaf + 1, NL), lax.rem(me_leaf + NL - 1, NL)
    pl.semaphore_signal(barrier, inc=1, device_id=(up, me), device_id_type=MESH)
    pl.semaphore_signal(barrier, inc=1, device_id=(down, me), device_id_type=MESH)
    for t in range(1, NO):
        pl.semaphore_signal(barrier, inc=1, device_id=(me_leaf, lax.rem(me + t, NO)), device_id_type=MESH)

    reaches = [1 << i for i in range(max(NL // 4, 1).bit_length())]

    def tell(i):
        d = reaches[i]
        for to in (lax.rem(me_leaf + d, NL), lax.rem(me_leaf + NL - d, NL)):
            pl.semaphore_signal(known.at[i], inc=1, device_id=(to, me), device_id_type=MESH)

    def hear(i):
        pl.semaphore_wait(known.at[i], 2)

    def tell_orbs():
        for t in range(1, NO):
            pl.semaphore_signal(
                known.at[len(reaches)], inc=1, device_id=(me_leaf, lax.rem(me + t, NO)), device_id_type=MESH)

    for load in loads[1:]:
        load.start()
    pair_load.start()

    small[0].wait()
    small[1].wait()
    count = counts[me_leaf]

    def make_product(c):
        loads[c].wait()

        def block(g):
            value = orb_v[c][g].astype(F32) * potential[g].astype(F32)[None]
            return value.astype(BF16).reshape(RO, PP)

        for g in range(SL):
            pools[c][g] = block(g)
        pools[c][SL + 4] = jnp.zeros((RO, PP), BF16)
        for j in range(2):
            staged[c, j] = block(jnp.maximum(count - 2 + j, 0))

    def exchange(c):
        to_up = pltpu.make_async_remote_copy(
            src_ref=staged.at[c], dst_ref=pools[c].at[SL:SL + 2], send_sem=ex_send.at[c, 0],
            recv_sem=ex_recv.at[c, 0], device_id=(up, me), device_id_type=MESH)
        to_down = pltpu.make_async_remote_copy(
            src_ref=pools[c].at[0:2], dst_ref=pools[c].at[SL + 2:SL + 4], send_sem=ex_send.at[c, 1],
            recv_sem=ex_recv.at[c, 1], device_id=(down, me), device_id_type=MESH)
        return to_up, to_down

    exchanges = [exchange(c) for c in range(NC)]

    def start_exchange(c):
        for copy in exchanges[c]:
            copy.start()

    make_product(0)
    pl.semaphore_wait(barrier, NO - 1 + 2)
    start_exchange(0)
    tell(0)
    for c in range(1, NC):
        make_product(c)

    small[2].wait()
    small[3].wait()
    count_low = counts[down]
    for g in range(SL):
        live[g] = (g < count).astype(jnp.int32)
        for d in range(6):
            own, at = owner[g, d], slot[g, d]
            low = SL + jnp.clip(at - count_low + 2, 0, 1)
            high = SL + 2 + jnp.clip(at, 0, 1)
            here = jnp.clip(at, 0, SL - 1)
            place = jnp.where(own == me_leaf, here, jnp.where(own < me_leaf, low, high))
            table[d * SL + g] = jnp.where(own < 0, SL + 4, place)

    TD = T * D
    lanes = T * RO
    rise = (split(iota((RO, D), 0), CO)[0] == iota((RO, D), 1)).astype(BF16)
    term_a, depth_a = split(iota((TD, lanes), 0), D)
    term_b, rest_b = split(iota((TD, lanes), 1), RO)
    widen = ((term_a == term_b) & (depth_a == split(rest_b, D)[1])).astype(BF16)
    same = split(iota((RO, lanes), 0), CO)[1] == split(split(iota((RO, lanes), 1), RO)[1], D)[0]

    small[4].wait()
    for d in range(7):
        tall = lax.dot_general(rise, axis[d], (((1,), (1,)), ((), ())), preferred_element_type=F32).astype(BF16)
        full_d = jnp.dot(tall, widen, preferred_element_type=F32)
        spread[:, d * lanes:(d + 1) * lanes] = jnp.where(same, full_d, 0.0).astype(BF16)

    pair_load.wait()
    QB = PP // T
    sort = reorder(QB, T)
    for d in range(7):
        for q in range(0, PP, QB):
            block = jnp.dot(sort, raw_v[d, q:q + QB].reshape(PP, PP), preferred_element_type=F32).astype(BF16)
            for r in range(T):
                pair_v[d, r, q:q + QB] = block[r * QB:(r + 1) * QB]

    def pair_step(c, d, slots):
        first = slots[0]
        many = source.at[first * RO:(slots[-1] + 1) * RO]
        if d < 6:
            for g in slots:
                source[g * RO:(g + 1) * RO, :] = pools[c][table[d * SL + g]]
        for r in range(T):
            left = many[...] if d < 6 else pools[c][first:slots[-1] + 1].reshape(len(slots) * RO, PP)
            value = jnp.dot(left, pair_v[d, r], preferred_element_type=F32).astype(BF16)
            for i, g in enumerate(slots):
                inner[c % 2, g, d, r] = value[i * RO:(i + 1) * RO]

    rows = ZD * CO

    def between(c, g, here, there, peer):
        at = pl.ds(0, SL * rows) if c < NC - 1 else pl.ds(g * rows, rows)
        return pltpu.make_async_remote_copy(
            src_ref=send1.at[c, there, at], dst_ref=recv1.at[here, c, at], send_sem=a_send.at[c + g, there],
            recv_sem=a_recv.at[c + g, here], device_id=(me_leaf, peer), device_id_type=MESH)

    def to_peer(c, t, g=0):
        peer = lax.rem(me + t, NO)
        return between(c, g, me, peer, peer)

    def from_peer(c, t, g=0):
        peer = lax.rem(me + NO - t, NO)
        return between(c, g, peer, peer, peer)

    def assemble(c):
        if c < NC - 1:
            for t in range(1, NO):
                from_peer(c, t).wait_recv()
        for g in range(SL):
            if c == NC - 1:
                for t in range(1, NO):
                    from_peer(c, t, g).wait_recv()
            block = recv1[:, c, g * rows:(g + 1) * rows, :].astype(F32).reshape(NO, ZD, CO, PP)
            for k in range(ZD):
                rows_v[g * ZD + k, c * NO * CO:(c + 1) * NO * CO, :] = (
                    block[:, k].reshape(NO * CO, PP).astype(BF16))

    every = tuple(range(SL))
    start_exchange(1)
    for c in range(2):
        pair_step(c, 6, every)
    for c in range(NC):
        for copy in exchanges[c]:
            copy.wait_recv()
        if c + 2 < NC:
            start_exchange(c + 2)
        for slots in (every,) if c < NC - 1 else (every[:3], every[3:]):
            for d in range(6 if c < 2 else 7):
                pair_step(c, d, slots)
            for g in slots:
                weights = inner[c % 2, g].reshape(7 * T * RO, PP)
                total = jnp.dot(spread[...], weights, preferred_element_type=F32)
                total = jnp.where(live[g] > 0, total, 0.0).astype(BF16)
                for j in range(NO):
                    send1[c, j, g * rows:(g + 1) * rows, :] = total[j * rows:(j + 1) * rows]
                if c == NC - 1:
                    for t in range(1, NO):
                        to_peer(c, t, g).start()
        if c < NC - 1:
            for t in range(1, NO):
                to_peer(c, t).start()
            for i in (2 * c, 2 * c + 1):
                if i < len(reaches):
                    hear(i)
                    if i + 1 < len(reaches):
                        tell(i + 1)
                    else:
                        tell_orbs()
        recv1[me, c] = send1[c, me]
        if c >= 1:
            assemble(c - 1)
    assemble(NC - 1)

    total = None
    for k in range(SL * ZD):
        block = rows_v[k]
        term = lax.dot_general(block, block, (((1,), (1,)), ((), ())), preferred_element_type=F32)
        total = term if total is None else total + term
    S[...] = total

    pl.semaphore_wait(known.at[len(reaches)], NO - 1)

    def p1(q_from, q_to, q_dev):
        return pltpu.make_async_remote_copy(
            src_ref=S.at[pl.ds(pl.multiple_of(q_to * PR, PR), PR)], dst_ref=part1.at[q_from],
            send_sem=p1_send.at[q_dev], recv_sem=p1_recv.at[q_from], device_id=member(q_dev), device_id_type=MESH)

    def p1_start(t, carry):
        q = lax.rem(m + t, G)
        p1(m, q, q).start()
        return carry

    lax.fori_loop(1, G, p1_start, 0)
    part1[m] = S[pl.ds(pl.multiple_of(m * PR, PR), PR)]

    def p1_wait(t, carry):
        q = lax.rem(m + G - t, G)
        p1(q, q, q).wait_recv()
        return carry

    lax.fori_loop(1, G, p1_wait, 0)
    part2[z] = jnp.sum(part1[...], axis=0)

    def p2(z_from, z_to):
        return pltpu.make_async_remote_copy(
            src_ref=part2.at[z_from], dst_ref=part2.at[z_from], send_sem=p2_send.at[z_to],
            recv_sem=p2_recv.at[z_from], device_id=(z_to * NX + x, me), device_id_type=MESH)

    for t in range(1, NZ):
        p2(z, lax.rem(z + t, NZ)).start()
    for t in range(1, NZ):
        other = lax.rem(z + NZ - t, NZ)
        p2(other, other).wait_recv()
    full[m] = jnp.sum(part2[...], axis=0)

    def p3(q_from, q_dev):
        return pltpu.make_async_remote_copy(
            src_ref=full.at[q_from], dst_ref=full.at[q_from], send_sem=p3_send.at[q_dev],
            recv_sem=p3_recv.at[q_from], device_id=member(q_dev), device_id_type=MESH)

    def p3_start(t, carry):
        q = lax.rem(m + t, G)
        p3(m, q).start()
        return carry

    lax.fori_loop(1, G, p3_start, 0)

    def p3_wait(t, carry):
        q = lax.rem(m + G - t, G)
        p3(q, q).wait_recv()
        return carry

    lax.fori_loop(1, G, p3_wait, 0)

    summed = full[...].reshape(N, N)
    diagonal = iota((N, N), 0) == iota((N, N), 1)
    trace = jnp.sum(jnp.sum(jnp.where(diagonal, summed, 0.0), axis=1, keepdims=True), axis=0, keepdims=True)
    scale = trace / N
    rotation = (jnp.where(diagonal, 1.5, 0.0) - 0.5 * summed / scale) / jnp.sqrt(scale)
    turn = jnp.transpose(rotation).astype(BF16)

    def back(g, a_from, a_to):
        return pltpu.make_async_remote_copy(
            src_ref=send2.at[a_to, g], dst_ref=recv2.at[a_from, g], send_sem=b_send.at[g, a_to],
            recv_sem=b_recv.at[g, a_from], device_id=(me_leaf, a_to), device_id_type=MESH)

    keeps = []
    for g in range(SL):
        for k in range(ZD):
            value = jnp.dot(turn, rows_v[g * ZD + k], preferred_element_type=F32).reshape(NC, NO, CO, PP)
            for s in range(NO):
                send2[s, g, k * OL:(k + 1) * OL, :] = value[:, s].reshape(OL, PP).astype(BF16)
        for t in range(1, NO):
            back(g, me, lax.rem(me + t, NO)).start()
        keeps.append(pltpu.make_async_copy(send2.at[me, g], recv2.at[me, g], out_sem.at[g]))
        keeps[-1].start()

    for g in range(SL):
        for t in range(1, NO):
            other = lax.rem(me + NO - t, NO)
            back(g, other, other).wait_recv()

    for pairs in exchanges:
        for copy in pairs:
            copy.wait_send()
    for c in range(NC):
        for g in range(SL if c == NC - 1 else 1):
            for t in range(1, NO):
                to_peer(c, t, g).wait_send()

    def drain(t, carry):
        q = lax.rem(m + t, G)
        p1(m, q, q).wait_send()
        p3(m, q).wait_send()
        return carry

    lax.fori_loop(1, G, drain, 0)
    for t in range(1, NZ):
        p2(z, lax.rem(z + t, NZ)).wait_send()
    for g in range(SL):
        for t in range(1, NO):
            back(g, me, lax.rem(me + t, NO)).wait_send()
    for keep in keeps:
        keep.wait()


def settle(dims, blocks, out, held, placed, in_sem, out_sem):
    NL, NX, NO, SL, OL, D, PP, T = dims
    loads = [pltpu.make_async_copy(blocks.at[:, g], held.at[g], in_sem.at[g]) for g in range(SL)]
    stores = [pltpu.make_async_copy(placed.at[g], out.at[g], out_sem.at[g]) for g in range(SL)]
    for load in loads:
        load.start()
    swap = reorder(D, 16)
    for g in range(SL):
        loads[g].wait()
        for h in range(OL // 16):
            block = held[g].reshape(NO, D // NO, OL // 16, 16, PP)[:, :, h].reshape(D * 16, PP)
            value = jnp.dot(swap, block, preferred_element_type=F32).astype(BF16)
            placed[g, h * 16:(h + 1) * 16] = value.reshape(16, D, PP)
        stores[g].start()
    for store in stores:
        store.wait()


def on_device(dims, orbitals, potential, counts, owner, slot, pair, axis):
    NL, NX, NO, SL, OL, D, PP, T = dims
    NC, NZ, G = OL // CO, NL // NX, NX * NO
    ZD, RO, N = D // NO, CO * D, OL * NO
    PR = N // G
    anywhere = pl.BlockSpec(memory_space=pl.ANY)
    dma = pltpu.SemaphoreType.DMA
    blocks = pl.pallas_call(
        functools.partial(kernel, dims),
        out_shape=jax.ShapeDtypeStruct((NO, SL, ZD * OL, PP), BF16),
        in_specs=[anywhere] * 7,
        out_specs=anywhere,
        scratch_shapes=[
            pltpu.SMEM((NL,), jnp.int32),
            pltpu.SMEM((SL, 6), jnp.int32),
            pltpu.SMEM((SL, 6), jnp.int32),
            pltpu.VMEM((SL, D, PP), BF16),
            pltpu.VMEM((7, T * D, D), BF16),
            pltpu.SMEM((6 * SL,), jnp.int32),
            pltpu.SMEM((SL,), jnp.int32),
            pltpu.VMEM((7, PP, T, PP), BF16),
            pltpu.VMEM((7, T, PP, PP), BF16),
            pltpu.VMEM((NC, 2, RO, PP), BF16),
            pltpu.VMEM((RO, 7 * T * RO), BF16),
            pltpu.VMEM((2, SL, 7, T, RO, PP), BF16),
            pltpu.VMEM((SL * RO, PP), BF16),
            pltpu.VMEM((NC, NO, SL * ZD * CO, PP), BF16),
            pltpu.VMEM((NO, NC, SL * ZD * CO, PP), BF16),
            pltpu.VMEM((SL * ZD, N, PP), BF16),
            pltpu.VMEM((N, N), F32),
            pltpu.VMEM((G, PR, N), F32),
            pltpu.VMEM((NZ, PR, N), F32),
            pltpu.VMEM((G, PR, N), F32),
            pltpu.VMEM((NO, SL, ZD * OL, PP), BF16),
            *[pltpu.VMEM((SL + 5, RO, PP), BF16) for _ in range(NC)],
            *[pltpu.VMEM((SL, CO, D, PP), BF16) for _ in range(NC)],
            dma((NC,)), dma(()), dma((NC, 2)), dma((NC, 2)),
            dma((NC - 1 + SL, NO)), dma((NC - 1 + SL, NO)),
            dma((G,)), dma((G,)), dma((NZ,)), dma((NZ,)), dma((G,)), dma((G,)),
            dma((SL, NO)), dma((SL, NO)), dma((SL,)), dma((5,)), pltpu.SemaphoreType.REGULAR((8,)),
        ],
        compiler_params=pltpu.CompilerParams(
            collective_id=0, has_side_effects=True, vmem_limit_bytes=56 * 2**20),
    )(counts, owner, slot, potential, axis.reshape(7, T * D, D), orbitals, pair)
    return pl.pallas_call(
        functools.partial(settle, dims),
        out_shape=jax.ShapeDtypeStruct(orbitals.shape, BF16),
        in_specs=[anywhere],
        out_specs=anywhere,
        scratch_shapes=[
            pltpu.VMEM((SL, NO, ZD * OL, PP), BF16),
            pltpu.VMEM((SL, OL, D, PP), BF16),
            dma((SL,)), dma((SL,)),
        ],
    )(blocks)


def solution(mesh):
    leaf, orb = mesh.shape["leaf"], mesh.shape["orb"]
    along_x = 4 if leaf % 4 == 0 and leaf > 4 else 2

    def step(orbitals, potential, counts, owner, slot, pair, axis):
        slots, orbs, depth, paired = orbitals.shape
        dims = (leaf, along_x, orb, slots, orbs, depth, paired, pair.shape[2])
        return on_device(dims, orbitals, potential, counts, owner, slot, pair, axis)

    placed = (
        P("leaf", "orb", None, None),
        P("leaf", None, None),
        P(),
        P("leaf", None),
        P("leaf", None),
        P(),
        P(),
    )
    return jax.shard_map(
        step,
        mesh=mesh,
        in_specs=placed,
        out_specs=P("leaf", "orb", None, None),
        check_vma=False,
    )
```

```python
import functools

import jax
import jax.numpy as jnp
from jax import lax
from jax.experimental import pallas as pl
from jax.experimental.pallas import tpu as pltpu
from jax.sharding import PartitionSpec as P

MESH = pl.DeviceIdType.MESH
F32 = jnp.float32
BF16 = jnp.bfloat16
CO = 8


def iota(shape, dim):
    return lax.broadcasted_iota(jnp.int32, shape, dim)


def split(value, size):
    return value >> (size.bit_length() - 1), value & (size - 1)


def reorder(outer, inner):
    size = outer * inner
    high, low = split(iota((size, size), 0), outer)
    other_high, other_low = split(iota((size, size), 1), inner)
    return ((high == other_low) & (low == other_high)).astype(BF16)


def kernel(
    dims,
    counts_in, owner_in, slot_in, potential_in, axis_in, orbitals, pair, recv2,
    counts, owner, slot, potential, axis, table, live, raw_v, pair_v, staged, spread, inner, source, send1, recv1, rows_v, S, part1, part2, full,
    send2, *rest,
):
    NL, NX, NO, SL, OL, D, PP, T = dims
    NC, NZ, G = OL // CO, NL // NX, NX * NO
    ZD = D // NO
    RO = CO * D
    N = OL * NO
    PR = N // G
    pools, orb_v = rest[:NC], rest[NC:2 * NC]
    (ld_sem, pair_sem, ex_send, ex_recv, a_send, a_recv, p1_send, p1_recv, p2_send, p2_recv, p3_send, p3_recv,
     b_send, b_recv, out_sem, small_sem, known) = rest[2 * NC:]
    me_leaf, me = lax.axis_index("leaf"), lax.axis_index("orb")
    x, z = lax.rem(me_leaf, NX), me_leaf // NX
    m = x * NO + me

    loads = [
        pltpu.make_async_copy(orbitals.at[:, c * CO:(c + 1) * CO], orb_v[c], ld_sem.at[c])
        for c in range(NC)
    ]
    pair_load = pltpu.make_async_copy(pair, raw_v, pair_sem)
    small = [
        pltpu.make_async_copy(*ends, small_sem.at[i])
        for i, ends in enumerate(
            ((counts_in, counts), (potential_in, potential), (owner_in, owner), (slot_in, slot), (axis_in, axis)))
    ]
    loads[0].start()
    for load in small:
        load.start()

    def member(q):
        return (z * NX + q // NO, lax.rem(q, NO))

    barrier = pltpu.get_barrier_semaphore()
    up, down = lax.rem(me_leaf + 1, NL), lax.rem(me_leaf + NL - 1, NL)
    pl.semaphore_signal(barrier, inc=1, device_id=(up, me), device_id_type=MESH)
    pl.semaphore_signal(barrier, inc=1, device_id=(down, me), device_id_type=MESH)
    for t in range(1, NO):
        pl.semaphore_signal(barrier, inc=1, device_id=(me_leaf, lax.rem(me + t, NO)), device_id_type=MESH)

    reaches = [1 << i for i in range(max(NL // 4, 1).bit_length())]

    def tell(i):
        d = reaches[i]
        for to in (lax.rem(me_leaf + d, NL), lax.rem(me_leaf + NL - d, NL)):
            pl.semaphore_signal(known.at[i], inc=1, device_id=(to, me), device_id_type=MESH)

    def hear(i):
        pl.semaphore_wait(known.at[i], 2)

    def tell_orbs():
        for t in range(1, NO):
            pl.semaphore_signal(
                known.at[len(reaches)], inc=1, device_id=(me_leaf, lax.rem(me + t, NO)), device_id_type=MESH)

    for load in loads[1:]:
        load.start()
    pair_load.start()

    small[0].wait()
    small[1].wait()
    count = counts[me_leaf]

    def make_product(c):
        loads[c].wait()

        def block(g):
            value = orb_v[c][g].astype(F32) * potential[g].astype(F32)[None]
            return value.astype(BF16).reshape(RO, PP)

        for g in range(SL):
            pools[c][g] = block(g)
        pools[c][SL + 4] = jnp.zeros((RO, PP), BF16)
        for j in range(2):
            staged[c, j] = block(jnp.maximum(count - 2 + j, 0))

    def exchange(c):
        to_up = pltpu.make_async_remote_copy(
            src_ref=staged.at[c], dst_ref=pools[c].at[SL:SL + 2], send_sem=ex_send.at[c, 0],
            recv_sem=ex_recv.at[c, 0], device_id=(up, me), device_id_type=MESH)
        to_down = pltpu.make_async_remote_copy(
            src_ref=pools[c].at[0:2], dst_ref=pools[c].at[SL + 2:SL + 4], send_sem=ex_send.at[c, 1],
            recv_sem=ex_recv.at[c, 1], device_id=(down, me), device_id_type=MESH)
        return to_up, to_down

    exchanges = [exchange(c) for c in range(NC)]

    def start_exchange(c):
        for copy in exchanges[c]:
            copy.start()

    make_product(0)
    pl.semaphore_wait(barrier, NO - 1 + 2)
    start_exchange(0)
    tell(0)
    for c in range(1, NC):
        make_product(c)

    small[2].wait()
    small[3].wait()
    count_low = counts[down]
    for g in range(SL):
        live[g] = (g < count).astype(jnp.int32)
        for d in range(6):
            own, at = owner[g, d], slot[g, d]
            low = SL + jnp.clip(at - count_low + 2, 0, 1)
            high = SL + 2 + jnp.clip(at, 0, 1)
            here = jnp.clip(at, 0, SL - 1)
            place = jnp.where(own == me_leaf, here, jnp.where(own < me_leaf, low, high))
            table[d * SL + g] = jnp.where(own < 0, SL + 4, place)

    TD = T * D
    lanes = T * RO
    rise = (split(iota((RO, D), 0), CO)[0] == iota((RO, D), 1)).astype(BF16)
    term_a, depth_a = split(iota((TD, lanes), 0), D)
    term_b, rest_b = split(iota((TD, lanes), 1), RO)
    widen = ((term_a == term_b) & (depth_a == split(rest_b, D)[1])).astype(BF16)
    same = split(iota((RO, lanes), 0), CO)[1] == split(split(iota((RO, lanes), 1), RO)[1], D)[0]

    small[4].wait()
    for d in range(7):
        tall = lax.dot_general(rise, axis[d], (((1,), (1,)), ((), ())), preferred_element_type=F32).astype(BF16)
        full_d = jnp.dot(tall, widen, preferred_element_type=F32)
        spread[:, d * lanes:(d + 1) * lanes] = jnp.where(same, full_d, 0.0).astype(BF16)

    pair_load.wait()
    QB = PP // T
    sort = reorder(QB, T)
    for d in range(7):
        for q in range(0, PP, QB):
            block = jnp.dot(sort, raw_v[d, q:q + QB].reshape(PP, PP), preferred_element_type=F32).astype(BF16)
            for r in range(T):
                pair_v[d, r, q:q + QB] = block[r * QB:(r + 1) * QB]

    def pair_step(c, d, slots):
        first = slots[0]
        many = source.at[first * RO:(slots[-1] + 1) * RO]
        if d < 6:
            for g in slots:
                source[g * RO:(g + 1) * RO, :] = pools[c][table[d * SL + g]]
        for r in range(T):
            left = many[...] if d < 6 else pools[c][first:slots[-1] + 1].reshape(len(slots) * RO, PP)
            value = jnp.dot(left, pair_v[d, r], preferred_element_type=F32).astype(BF16)
            for i, g in enumerate(slots):
                inner[c % 2, g, d, r] = value[i * RO:(i + 1) * RO]

    rows = ZD * CO

    def between(c, g, here, there, peer):
        at = pl.ds(0, SL * rows) if c < NC - 1 else pl.ds(g * rows, rows)
        return pltpu.make_async_remote_copy(
            src_ref=send1.at[c, there, at], dst_ref=recv1.at[here, c, at], send_sem=a_send.at[c + g, there],
            recv_sem=a_recv.at[c + g, here], device_id=(me_leaf, peer), device_id_type=MESH)

    def to_peer(c, t, g=0):
        peer = lax.rem(me + t, NO)
        return between(c, g, me, peer, peer)

    def from_peer(c, t, g=0):
        peer = lax.rem(me + NO - t, NO)
        return between(c, g, peer, peer, peer)

    def assemble(c, each=None):
        if c < NC - 1:
            for t in range(1, NO):
                from_peer(c, t).wait_recv()
        for g in range(SL):
            if c == NC - 1:
                for t in range(1, NO):
                    from_peer(c, t, g).wait_recv()
            block = recv1[:, c, g * rows:(g + 1) * rows, :].astype(F32).reshape(NO, ZD, CO, PP)
            for k in range(ZD):
                rows_v[g * ZD + k, c * NO * CO:(c + 1) * NO * CO, :] = (
                    block[:, k].reshape(NO * CO, PP).astype(BF16))
            if each is not None:
                each(g)

    every = tuple(range(SL))
    start_exchange(1)
    for c in range(2):
        pair_step(c, 6, every)
    for c in range(NC):
        for copy in exchanges[c]:
            copy.wait_recv()
        if c + 2 < NC:
            start_exchange(c + 2)
        for slots in (every,) if c < NC - 1 else (every[:3], every[3:]):
            for d in range(6 if c < 2 else 7):
                pair_step(c, d, slots)
            for g in slots:
                weights = inner[c % 2, g].reshape(7 * T * RO, PP)
                total = jnp.dot(spread[...], weights, preferred_element_type=F32)
                total = jnp.where(live[g] > 0, total, 0.0).astype(BF16)
                for j in range(NO):
                    send1[c, j, g * rows:(g + 1) * rows, :] = total[j * rows:(j + 1) * rows]
                if c == NC - 1:
                    for t in range(1, NO):
                        to_peer(c, t, g).start()
        if c < NC - 1:
            for t in range(1, NO):
                to_peer(c, t).start()
            for i in (2 * c, 2 * c + 1):
                if i < len(reaches):
                    hear(i)
                    if i + 1 < len(reaches):
                        tell(i + 1)
                    else:
                        tell_orbs()
        recv1[me, c] = send1[c, me]
        if c >= 1:
            assemble(c - 1)

    def intersect(g):
        total = S[...] if g else None
        for k in range(g * ZD, (g + 1) * ZD):
            block = rows_v[k]
            term = lax.dot_general(block, block, (((1,), (1,)), ((), ())), preferred_element_type=F32)
            total = term if total is None else total + term
        S[...] = total

    assemble(NC - 1, intersect)

    pl.semaphore_wait(known.at[len(reaches)], NO - 1)

    def p1(q_from, q_to, q_dev):
        return pltpu.make_async_remote_copy(
            src_ref=S.at[pl.ds(pl.multiple_of(q_to * PR, PR), PR)], dst_ref=part1.at[q_from],
            send_sem=p1_send.at[q_dev], recv_sem=p1_recv.at[q_from], device_id=member(q_dev), device_id_type=MESH)

    def p1_start(t, carry):
        q = lax.rem(m + t, G)
        p1(m, q, q).start()
        return carry

    lax.fori_loop(1, G, p1_start, 0)
    part1[m] = S[pl.ds(pl.multiple_of(m * PR, PR), PR)]

    def p1_wait(t, carry):
        q = lax.rem(m + G - t, G)
        p1(q, q, q).wait_recv()
        return carry

    lax.fori_loop(1, G, p1_wait, 0)
    part2[z] = jnp.sum(part1[...], axis=0)

    def p2(z_from, z_to):
        return pltpu.make_async_remote_copy(
            src_ref=part2.at[z_from], dst_ref=part2.at[z_from], send_sem=p2_send.at[z_to],
            recv_sem=p2_recv.at[z_from], device_id=(z_to * NX + x, me), device_id_type=MESH)

    for t in range(1, NZ):
        p2(z, lax.rem(z + t, NZ)).start()
    for t in range(1, NZ):
        other = lax.rem(z + NZ - t, NZ)
        p2(other, other).wait_recv()
    full[m] = jnp.sum(part2[...], axis=0)

    def p3(q_from, q_dev):
        return pltpu.make_async_remote_copy(
            src_ref=full.at[q_from], dst_ref=full.at[q_from], send_sem=p3_send.at[q_dev],
            recv_sem=p3_recv.at[q_from], device_id=member(q_dev), device_id_type=MESH)

    def p3_start(t, carry):
        q = lax.rem(m + t, G)
        p3(m, q).start()
        return carry

    lax.fori_loop(1, G, p3_start, 0)

    def p3_wait(t, carry):
        q = lax.rem(m + G - t, G)
        p3(q, q).wait_recv()
        return carry

    lax.fori_loop(1, G, p3_wait, 0)

    summed = full[...].reshape(N, N)
    diagonal = iota((N, N), 0) == iota((N, N), 1)
    trace = jnp.sum(jnp.sum(jnp.where(diagonal, summed, 0.0), axis=1, keepdims=True), axis=0, keepdims=True)
    scale = trace / N
    rotation = (jnp.where(diagonal, 1.5, 0.0) - 0.5 * summed / scale) / jnp.sqrt(scale)
    turn = jnp.transpose(rotation).astype(BF16)

    def back(g, a_from, a_to):
        return pltpu.make_async_remote_copy(
            src_ref=send2.at[a_to, g], dst_ref=recv2.at[a_from, g], send_sem=b_send.at[g, a_to],
            recv_sem=b_recv.at[g, a_from], device_id=(me_leaf, a_to), device_id_type=MESH)

    keeps = []
    for g in range(SL):
        for k in range(ZD):
            value = jnp.dot(turn, rows_v[g * ZD + k], preferred_element_type=F32).reshape(NC, NO, CO, PP)
            for s in range(NO):
                send2[s, g, k * OL:(k + 1) * OL, :] = value[:, s].reshape(OL, PP).astype(BF16)
        for t in range(1, NO):
            back(g, me, lax.rem(me + t, NO)).start()
        keeps.append(pltpu.make_async_copy(send2.at[me, g], recv2.at[me, g], out_sem.at[g]))
        keeps[-1].start()

    for g in range(SL):
        for t in range(1, NO):
            other = lax.rem(me + NO - t, NO)
            back(g, other, other).wait_recv()

    for pairs in exchanges:
        for copy in pairs:
            copy.wait_send()
    for c in range(NC):
        for g in range(SL if c == NC - 1 else 1):
            for t in range(1, NO):
                to_peer(c, t, g).wait_send()

    def drain(t, carry):
        q = lax.rem(m + t, G)
        p1(m, q, q).wait_send()
        p3(m, q).wait_send()
        return carry

    lax.fori_loop(1, G, drain, 0)
    for t in range(1, NZ):
        p2(z, lax.rem(z + t, NZ)).wait_send()
    for g in range(SL):
        for t in range(1, NO):
            back(g, me, lax.rem(me + t, NO)).wait_send()
    for keep in keeps:
        keep.wait()


def settle(dims, blocks, out, held, placed, in_sem, out_sem):
    NL, NX, NO, SL, OL, D, PP, T = dims
    loads = [pltpu.make_async_copy(blocks.at[:, g], held.at[g], in_sem.at[g]) for g in range(SL)]
    stores = [pltpu.make_async_copy(placed.at[g], out.at[g], out_sem.at[g]) for g in range(SL)]
    for load in loads:
        load.start()
    swap = reorder(D, 16)
    for g in range(SL):
        loads[g].wait()
        for h in range(OL // 16):
            block = held[g].reshape(NO, D // NO, OL // 16, 16, PP)[:, :, h].reshape(D * 16, PP)
            value = jnp.dot(swap, block, preferred_element_type=F32).astype(BF16)
            placed[g, h * 16:(h + 1) * 16] = value.reshape(16, D, PP)
        stores[g].start()
    for store in stores:
        store.wait()


def on_device(dims, orbitals, potential, counts, owner, slot, pair, axis):
    NL, NX, NO, SL, OL, D, PP, T = dims
    NC, NZ, G = OL // CO, NL // NX, NX * NO
    ZD, RO, N = D // NO, CO * D, OL * NO
    PR = N // G
    anywhere = pl.BlockSpec(memory_space=pl.ANY)
    dma = pltpu.SemaphoreType.DMA
    blocks = pl.pallas_call(
        functools.partial(kernel, dims),
        out_shape=jax.ShapeDtypeStruct((NO, SL, ZD * OL, PP), BF16),
        in_specs=[anywhere] * 7,
        out_specs=anywhere,
        scratch_shapes=[
            pltpu.SMEM((NL,), jnp.int32),
            pltpu.SMEM((SL, 6), jnp.int32),
            pltpu.SMEM((SL, 6), jnp.int32),
            pltpu.VMEM((SL, D, PP), BF16),
            pltpu.VMEM((7, T * D, D), BF16),
            pltpu.SMEM((6 * SL,), jnp.int32),
            pltpu.SMEM((SL,), jnp.int32),
            pltpu.VMEM((7, PP, T, PP), BF16),
            pltpu.VMEM((7, T, PP, PP), BF16),
            pltpu.VMEM((NC, 2, RO, PP), BF16),
            pltpu.VMEM((RO, 7 * T * RO), BF16),
            pltpu.VMEM((2, SL, 7, T, RO, PP), BF16),
            pltpu.VMEM((SL * RO, PP), BF16),
            pltpu.VMEM((NC, NO, SL * ZD * CO, PP), BF16),
            pltpu.VMEM((NO, NC, SL * ZD * CO, PP), BF16),
            pltpu.VMEM((SL * ZD, N, PP), BF16),
            pltpu.VMEM((N, N), F32),
            pltpu.VMEM((G, PR, N), F32),
            pltpu.VMEM((NZ, PR, N), F32),
            pltpu.VMEM((G, PR, N), F32),
            pltpu.VMEM((NO, SL, ZD * OL, PP), BF16),
            *[pltpu.VMEM((SL + 5, RO, PP), BF16) for _ in range(NC)],
            *[pltpu.VMEM((SL, CO, D, PP), BF16) for _ in range(NC)],
            dma((NC,)), dma(()), dma((NC, 2)), dma((NC, 2)),
            dma((NC - 1 + SL, NO)), dma((NC - 1 + SL, NO)),
            dma((G,)), dma((G,)), dma((NZ,)), dma((NZ,)), dma((G,)), dma((G,)),
            dma((SL, NO)), dma((SL, NO)), dma((SL,)), dma((5,)), pltpu.SemaphoreType.REGULAR((8,)),
        ],
        compiler_params=pltpu.CompilerParams(
            collective_id=0, has_side_effects=True, vmem_limit_bytes=56 * 2**20),
    )(counts, owner, slot, potential, axis.reshape(7, T * D, D), orbitals, pair)
    return pl.pallas_call(
        functools.partial(settle, dims),
        out_shape=jax.ShapeDtypeStruct(orbitals.shape, BF16),
        in_specs=[anywhere],
        out_specs=anywhere,
        scratch_shapes=[
            pltpu.VMEM((SL, NO, ZD * OL, PP), BF16),
            pltpu.VMEM((SL, OL, D, PP), BF16),
            dma((SL,)), dma((SL,)),
        ],
    )(blocks)


def solution(mesh):
    leaf, orb = mesh.shape["leaf"], mesh.shape["orb"]
    along_x = 4 if leaf % 4 == 0 and leaf > 4 else 2

    def step(orbitals, potential, counts, owner, slot, pair, axis):
        slots, orbs, depth, paired = orbitals.shape
        dims = (leaf, along_x, orb, slots, orbs, depth, paired, pair.shape[2])
        return on_device(dims, orbitals, potential, counts, owner, slot, pair, axis)

    placed = (
        P("leaf", "orb", None, None),
        P("leaf", None, None),
        P(),
        P("leaf", None),
        P("leaf", None),
        P(),
        P(),
    )
    return jax.shard_map(
        step,
        mesh=mesh,
        in_specs=placed,
        out_specs=P("leaf", "orb", None, None),
        check_vma=False,
    )
```
